32 devices in a mesh: dp: 8 (over z, y), fsdp: 4 (over x, core).
Axes of the slice: x: 2, y: 2, z: 4, core: 2. Of those that a mesh axis runs over, the one named last changes fastest.
Arguments:
- feats: bfloat16 [8, 4, 8, 128, 256], P('dp', 'fsdp'), may hold values from -6 to 6
- grad_out: bfloat16 [8, 4, 8, 128, 256], P('dp', 'fsdp'), may hold values from -6 to 6
- kernel: bfloat16 [27, 256, 256], P(None, 'fsdp'), may hold values from -0.25 to 0.25
- send_bricks: int32 [8, 4, 8, 2], P('dp', 'fsdp'), may hold values from -1 to 7, as said below
- kmap: int32 [8, 4, 27, 2, 3], P('dp', 'fsdp'), may hold values from 0 to 23, as said below
- pair_count: int32 [8, 4, 27], P('dp', 'fsdp'), may hold values from 1 to 3, as said below
Outputs:
- out_feats: bfloat16 [8, 4, 8, 128, 256], P('dp', 'fsdp')
- in_grad: bfloat16 [8, 4, 8, 128, 256], P('dp', 'fsdp')
- kernel_grad: float32 [27, 256, 256], P(None, 'fsdp')
The draws below stay inside these ranges and needn't reach their ends.
Inputs may be any that keep to these rules, and one draw needn't show every extreme that they name: `send_bricks`: entry (d, f, p, c) names the brick of device (d, f) sent to device (p, f) in slot c, or -1 for an empty slot. A device sends nothing to itself, fills exactly 6 slots, and fills both slots of at least one peer. kmap[d, f, t, 0, s] is an input brick of pool[d, f]: below 8 an own brick, else received slot p * 2 + c after the 8 own ones, and then always a slot that its sender filled. kmap[d, f, t, 1, s] is an output brick, below 8. Slots that are not live hold such ids too. `pair_count`: on some device every offset has 3 live slots.
All inputs are finite; a program needn't handle non-finite values.
Results may differ from the reference program's by a relative error of at most 0.0046.
Values may be sent and summed in bfloat16 or wider, within the bound.
A program may use at most 192 MiB of HBM per device.

```python
import jax
import jax.numpy as jnp
from jax import lax

C = 256
TAPS = 27
BRICK = 128
CAP = 2
SLOTS = 3
BR = 8
PEERS = 8
COLUMNS = 4
GHOST = 6
POOL = 24
GRAD_DIV = 128
N_DP = 8
N_FSDP = 4


def shared_tables(key):
    base = jax.random.fold_in(key, 101)
    keys = jax.random.split(base, 9)
    span = (PEERS - 1) * CAP
    slot_ids = jnp.arange(span, dtype=jnp.int32)
    noise = jax.random.randint(keys[0], (PEERS, COLUMNS, span), 0, 2 ** 20)
    forced = jax.random.randint(keys[1], (PEERS, COLUMNS, 1), 0, PEERS - 1)
    score = jnp.where(slot_ids // CAP == forced, slot_ids - span, noise * span + slot_ids)
    order = jnp.argsort(score, axis=-1)
    ranks = jnp.argsort(order, axis=-1)
    chosen = ranks < GHOST
    bricks = jax.random.randint(keys[2], (PEERS, COLUMNS, span), 0, BR)
    picked = jnp.where(chosen, bricks, -1).astype(jnp.int32)
    sender = jnp.arange(PEERS)[:, None, None]
    target = jnp.arange(PEERS)[None, :, None]
    within = jnp.arange(CAP)[None, None, :]
    offset = (target - sender - 1) % PEERS
    valid = offset < PEERS - 1
    safe_index = jnp.where(valid, offset * CAP + within, 0)
    picked_t = jnp.transpose(picked, (0, 2, 1))
    table = picked_t[sender, safe_index]
    table = jnp.where(valid[:, :, :, None], table, -1)
    send = jnp.transpose(table, (0, 3, 1, 2)).astype(jnp.int32)
    filled = jnp.transpose(send, (2, 1, 0, 3)) >= 0
    fill_flat = filled.reshape(PEERS, COLUMNS, PEERS * CAP)
    fill_total = jnp.sum(fill_flat.astype(jnp.int32), axis=-1)
    ghost_order = jnp.argsort(jnp.where(fill_flat, 0, 1) * (PEERS * CAP) + jnp.arange(PEERS * CAP), axis=-1)
    valid_total = BR + fill_total
    choose = jax.random.randint(keys[3], (PEERS, COLUMNS, TAPS, SLOTS), 0, 2 ** 20) % valid_total[:, :, None, None]
    ghost_pos = jnp.clip(choose - BR, 0, PEERS * CAP - 1).reshape(PEERS, COLUMNS, TAPS * SLOTS)
    ghost_ids = BR + jnp.take_along_axis(ghost_order, ghost_pos, axis=-1).reshape(PEERS, COLUMNS, TAPS, SLOTS)
    source_ids = jnp.where(choose < BR, choose, ghost_ids)
    target_ids = jax.random.randint(keys[4], (PEERS, COLUMNS, TAPS, SLOTS), 0, BR)
    kernel_map = jnp.stack([source_ids, target_ids], axis=3).astype(jnp.int32)
    first = jax.random.randint(keys[5], (PEERS, COLUMNS), 0, SLOTS)
    second = jax.random.randint(keys[6], (PEERS, COLUMNS), 0, SLOTS)
    levels = 1 + first * second // SLOTS
    heavy = jax.random.randint(keys[7], (), 0, PEERS * COLUMNS)
    device_ids = jnp.arange(PEERS * COLUMNS).reshape(PEERS, COLUMNS)
    minus = jax.random.randint(keys[8], (PEERS, COLUMNS, TAPS), 0, 2)
    counts = jnp.maximum(1, levels[:, :, None] - minus)
    counts = jnp.where(device_ids[:, :, None] == heavy, SLOTS, counts).astype(jnp.int32)
    return (send, kernel_map, counts)


def draw_send_bricks(key, part):
    return shared_tables(key)[0]


def draw_kmap(key, part):
    return shared_tables(key)[1]


def draw_pair_count(key, part):
    return shared_tables(key)[2]


def block_scale(key, dims, pieces, low, high):
    def one(dim, parts):
        heights = jax.random.uniform(jax.random.fold_in(jax.random.fold_in(key, 6), dim), (parts,), jnp.float32, low / len(pieces), high / len(pieces))
        return jnp.repeat(jnp.exp(heights), dims[dim] // parts).reshape((-1,) + (1,) * (len(dims) - dim - 1))

    gain = one(*pieces[0])
    for cut in pieces[1:]:
        gain = gain * one(*cut)
    return gain


def normal_values(stream_key, extent, width, most, cuts=(), kind=jnp.bfloat16):
    entries = jax.random.normal(stream_key, extent, jnp.float32) * width
    if len(cuts) > 0:
        entries = block_scale(stream_key, extent, cuts, -0.22, 0.18) * entries
    return jnp.clip(entries, min=-most, max=most).astype(kind)


def setup_inputs(seed: int = 0) -> dict:
    key_list = jax.random.split(jax.random.key(seed), 7)
    feats = normal_values(key_list[0], (PEERS, COLUMNS, BR, BRICK, C), 1.0, 6.0, ((0, 8), (1, 4)))
    grad_out = normal_values(key_list[1], (PEERS, COLUMNS, BR, BRICK, C), 1.0, 6.0, ((0, 8), (1, 4)))
    kernel = normal_values(key_list[2], (TAPS, C, C), (2 * C) ** -0.5, 0.25, ((1, 4),))
    send_bricks = draw_send_bricks(jax.random.fold_in(key_list[6], 71), 0)
    kmap = draw_kmap(jax.random.fold_in(key_list[6], 71), 0)
    pair_count = draw_pair_count(jax.random.fold_in(key_list[6], 71), 0)
    return {"feats": feats, "grad_out": grad_out, "kernel": kernel, "send_bricks": send_bricks, "kmap": kmap, "pair_count": pair_count}


def device_terms(own_rows, upstream_rows, weights, incoming, source_map, target_map, counts):
    pool = jnp.concatenate([own_rows, incoming.reshape(-1, BRICK, C)], axis=0)
    active = (jnp.arange(SLOTS)[None, :] < counts[:, None]).astype(jnp.float32)
    inputs = pool[source_map].astype(jnp.float32) * active[:, :, None, None]
    upstream = upstream_rows[target_map].astype(jnp.float32) * active[:, :, None, None]
    contrib = jnp.einsum('tsvc,tcd->tsvd', inputs, weights, precision=lax.Precision.HIGHEST)
    produced = jax.ops.segment_sum(contrib.reshape(TAPS * SLOTS, BRICK, C), target_map.reshape(-1), num_segments=BR)
    backward = jnp.einsum('tsvd,tcd->tsvc', upstream, weights, precision=lax.Precision.HIGHEST)
    pool_grad = jax.ops.segment_sum(backward.reshape(TAPS * SLOTS, BRICK, C), source_map.reshape(-1), num_segments=POOL)
    partial_value = jnp.einsum('tsvc,tsvd->tcd', inputs, upstream, precision=lax.Precision.HIGHEST)
    return produced, pool_grad, partial_value


def reference(feats, grad_out, kernel, send_bricks, kmap, pair_count):
    weights = kernel.astype(jnp.float32)
    peer_ids = jnp.arange(N_DP).astype(jnp.int32)
    produced_columns = []
    grad_columns = []
    kernel_sum = jnp.zeros((TAPS, C, C), jnp.float32)
    for column_index in range(N_FSDP):
        def advance(carry, receiver):
            input_sum, kernel_acc = carry
            senders = send_bricks[:, column_index, receiver, :]
            filled = (senders >= 0)
            incoming = feats[peer_ids[:, None], column_index, jnp.maximum(senders, 0)]
            incoming = incoming * filled[:, :, None, None].astype(jnp.bfloat16)
            produced, pool_grad, partial_value = device_terms(
                feats[receiver, column_index], grad_out[receiver, column_index], weights, incoming,
                kmap[receiver, column_index, :, 0, :], kmap[receiver, column_index, :, 1, :],
                pair_count[receiver, column_index])
            rounded = lax.optimization_barrier(pool_grad[BR:].astype(jnp.bfloat16))
            ghosts = rounded.astype(jnp.float32).reshape(N_DP, CAP, BRICK, C)
            input_sum = input_sum.at[receiver].add(pool_grad[:BR])
            owners = jnp.where(filled, senders, BR).astype(jnp.int32)
            input_sum = input_sum.at[peer_ids[:, None], owners].add(ghosts, mode="drop")
            return (input_sum, kernel_acc + partial_value), produced.astype(jnp.bfloat16)
        start = (jnp.zeros((N_DP, BR, BRICK, C), jnp.float32), jnp.zeros((TAPS, C, C), jnp.float32))
        (input_sum, kernel_acc), produced_all = lax.scan(advance, start, peer_ids)
        produced_columns.append(produced_all)
        grad_columns.append(input_sum.astype(jnp.bfloat16))
        kernel_sum = kernel_sum + kernel_acc
    out_feats = jnp.stack(produced_columns, axis=1)
    in_grad = jnp.stack(grad_columns, axis=1)
    kernel_grad = kernel_sum / jnp.float32(GRAD_DIV)
    return out_feats, in_grad, kernel_grad
```

```python
import jax
import jax.numpy as jnp
from jax import lax
from jax.experimental import pallas as pl
from jax.experimental.pallas import tpu as pltpu
from jax.sharding import PartitionSpec as P

F32 = jnp.float32
BF16 = jnp.bfloat16


def pair_kernel(kmap_ref, count_ref, own_ref, incoming_ref, upstream_ref, weights_ref,
                out_ref, ghost_ref, own_grad_ref, wgrad_ref,
                pool, out_acc, pool_acc, weights, sems):
    taps = weights.shape[0]
    slots = kmap_ref.shape[0] // (2 * taps)
    own_total = own_ref.shape[0]
    pool_total = pool.shape[0] - 1
    copies = [
        pltpu.make_async_copy(own_ref, pool.at[pl.ds(0, own_total)], sems.at[0]),
        pltpu.make_async_copy(incoming_ref, pool.at[pl.ds(own_total, pool_total - own_total)], sems.at[1]),
        pltpu.make_async_copy(weights_ref, weights, sems.at[2]),
    ]
    for copy in copies:
        copy.start()
    pool[pool_total] = jnp.zeros(pool.shape[1:], BF16)
    out_acc[...] = jnp.zeros_like(out_acc)
    pool_acc[...] = jnp.zeros_like(pool_acc)
    for copy in copies:
        copy.wait()

    def tap_step(t, carry):
        count = count_ref[t]
        sources, targets = [], []
        for s in range(slots):
            live = s < count
            sources.append(jnp.where(live, kmap_ref[t * 2 * slots + s], pool_total))
            targets.append(jnp.where(live, kmap_ref[t * 2 * slots + slots + s], own_total))
        inputs = jnp.concatenate([pool[i] for i in sources], axis=0)
        upstream = jnp.concatenate(
            [upstream_ref[jnp.minimum(o, own_total - 1)] for o in targets], axis=0)
        tap = weights[t]
        forward = jnp.dot(inputs, tap, preferred_element_type=F32)
        backward = lax.dot_general(upstream, tap, (((1,), (1,)), ((), ())), preferred_element_type=F32)
        wgrad = lax.dot_general(inputs, upstream, (((0,), (0,)), ((), ())), preferred_element_type=F32)
        wgrad_ref[t] = wgrad.astype(BF16)
        rows = pool.shape[1]
        for s in range(slots):
            out_acc[targets[s]] += forward[s * rows:(s + 1) * rows]
            pool_acc[sources[s]] += backward[s * rows:(s + 1) * rows]
        return carry

    lax.fori_loop(0, taps, tap_step, 0)
    out_ref[...] = out_acc[:own_total].astype(BF16)
    own_grad_ref[...] = pool_acc[:own_total]
    ghost_ref[...] = pool_acc[own_total:pool_total].astype(BF16)


def pair_products(kmap, counts, own, incoming, upstream, weights):
    own_total, rows, channels = own.shape
    ghost_total = incoming.shape[0]
    taps = weights.shape[0]
    pool_total = own_total + ghost_total
    smem = pl.BlockSpec(memory_space=pltpu.SMEM)
    vmem = pl.BlockSpec(memory_space=pltpu.VMEM)
    hbm = pl.BlockSpec(memory_space=pl.ANY)
    flops = 3 * 2 * kmap.size // 2 * rows * channels * channels
    return pl.pallas_call(
        pair_kernel,
        out_shape=(
            jax.ShapeDtypeStruct((own_total, rows, channels), BF16),
            jax.ShapeDtypeStruct((ghost_total, rows, channels), BF16),
            jax.ShapeDtypeStruct((own_total, rows, channels), F32),
            jax.ShapeDtypeStruct((taps, channels, channels), BF16),
        ),
        in_specs=[smem, smem, hbm, hbm, vmem, hbm],
        out_specs=(vmem, vmem, vmem, vmem),
        scratch_shapes=[
            pltpu.VMEM((pool_total + 1, rows, channels), BF16),
            pltpu.VMEM((own_total + 1, rows, channels), F32),
            pltpu.VMEM((pool_total + 1, rows, channels), F32),
            pltpu.VMEM((taps, channels, channels), BF16),
            pltpu.SemaphoreType.DMA((3,)),
        ],
        cost_estimate=pl.CostEstimate(flops=flops, bytes_accessed=16 * 2 ** 20, transcendentals=0),
        compiler_params=pltpu.CompilerParams(vmem_limit_bytes=58 * 2 ** 20),
        name="pair_products",
    )(kmap.reshape(-1), counts, own, incoming, upstream, weights)


def on_device(feats, grad_out, kernel, send_bricks, kmap, pair_count):
    own = feats[0, 0]
    senders = send_bricks[0, 0]
    peers, cap = senders.shape
    own_total, rows, channels = own.shape
    taps, depth, _ = kernel.shape
    filled = senders >= 0
    outgoing = own[jnp.maximum(senders, 0)] * filled[:, :, None, None].astype(BF16)
    incoming = lax.all_to_all(outgoing, "dp", split_axis=0, concat_axis=0, tiled=True)
    weights = lax.all_gather(kernel, "fsdp", axis=1, tiled=True)
    produced, ghosts, own_grad, wgrad = pair_products(
        kmap[0, 0], pair_count[0, 0], own, incoming.reshape(peers * cap, rows, channels),
        grad_out[0, 0], weights)
    returned = lax.all_to_all(
        ghosts.reshape(peers, cap, rows, channels), "dp", split_axis=0, concat_axis=0, tiled=True)
    chosen = (senders.reshape(1, -1) == jnp.arange(own_total)[:, None]).astype(BF16)
    back = jnp.einsum("bk,kvc->bvc", chosen, returned.reshape(peers * cap, rows, channels),
                      preferred_element_type=F32)
    in_grad = (own_grad + back).astype(BF16)
    divisor = F32(4 * lax.axis_size("dp") * lax.axis_size("fsdp"))
    portion = lax.psum_scatter(wgrad, "fsdp", scatter_dimension=1, tiled=True)
    portion = portion.reshape(taps * depth, channels)
    share = -(-taps * depth // (16 * peers)) * 16
    portion = jnp.pad(portion, ((0, share * peers - taps * depth), (0, 0)))
    pieces = lax.all_to_all(portion.reshape(peers, share, channels), "dp", 0, 0, tiled=True)
    total = jnp.sum(pieces.astype(F32), axis=0).astype(BF16)
    whole = lax.all_gather(total, "dp", axis=0, tiled=True)[:taps * depth]
    kernel_grad = whole.reshape(taps, depth, channels).astype(F32) / divisor
    return (produced[None, None], in_grad[None, None], kernel_grad)


def solution(mesh):
    bricks = P("dp", "fsdp", None, None, None)
    return jax.shard_map(
        on_device,
        mesh=mesh,
        in_specs=(bricks, bricks, P(None, "fsdp", None), P("dp", "fsdp", None, None),
                  P("dp", "fsdp", None, None, None), P("dp", "fsdp", None)),
        out_specs=(bricks, bricks, P(None, "fsdp", None)),
        check_vma=False,
    )
```

```python
import jax
import jax.numpy as jnp
from jax import lax
from jax.experimental import pallas as pl
from jax.experimental.pallas import tpu as pltpu
from jax.sharding import PartitionSpec as P

F32 = jnp.float32
BF16 = jnp.bfloat16


def pair_kernel(kmap_ref, count_ref, own_ref, incoming_ref, upstream_ref, weights_ref,
                out_ref, ghost_ref, own_grad_ref, wgrad_ref,
                pool, out_acc, pool_acc, weights, sems):
    taps = weights.shape[0]
    slots = kmap_ref.shape[0] // (2 * taps)
    own_total = own_ref.shape[0]
    pool_total = pool.shape[0] - 1
    copies = [
        pltpu.make_async_copy(own_ref, pool.at[pl.ds(0, own_total)], sems.at[0]),
        pltpu.make_async_copy(incoming_ref, pool.at[pl.ds(own_total, pool_total - own_total)], sems.at[1]),
        pltpu.make_async_copy(weights_ref, weights, sems.at[2]),
    ]
    for copy in copies:
        copy.start()
    pool[pool_total] = jnp.zeros(pool.shape[1:], BF16)
    out_acc[...] = jnp.zeros_like(out_acc)
    pool_acc[...] = jnp.zeros_like(pool_acc)
    for copy in copies:
        copy.wait()

    def tap_step(t, carry):
        count = count_ref[t]
        sources, targets = [], []
        for s in range(slots):
            live = s < count
            sources.append(jnp.where(live, kmap_ref[t * 2 * slots + s], pool_total))
            targets.append(jnp.where(live, kmap_ref[t * 2 * slots + slots + s], own_total))
        inputs = jnp.concatenate([pool[i] for i in sources], axis=0)
        upstream = jnp.concatenate(
            [upstream_ref[jnp.minimum(o, own_total - 1)] for o in targets], axis=0)
        tap = weights[t]
        forward = jnp.dot(inputs, tap, preferred_element_type=F32)
        backward = lax.dot_general(upstream, tap, (((1,), (1,)), ((), ())), preferred_element_type=F32)
        wgrad = lax.dot_general(inputs, upstream, (((0,), (0,)), ((), ())), preferred_element_type=F32)
        wgrad_ref[t] = wgrad.astype(BF16)
        rows = pool.shape[1]
        for s in range(slots):
            out_acc[targets[s]] += forward[s * rows:(s + 1) * rows]
            pool_acc[sources[s]] += backward[s * rows:(s + 1) * rows]
        return carry

    lax.fori_loop(0, taps, tap_step, 0)
    out_ref[...] = out_acc[:own_total].astype(BF16)
    own_grad_ref[...] = pool_acc[:own_total]
    ghost_ref[...] = pool_acc[own_total:pool_total].astype(BF16)


def pair_products(kmap, counts, own, incoming, upstream, weights):
    own_total, rows, channels = own.shape
    ghost_total = incoming.shape[0]
    taps = weights.shape[0]
    pool_total = own_total + ghost_total
    smem = pl.BlockSpec(memory_space=pltpu.SMEM)
    vmem = pl.BlockSpec(memory_space=pltpu.VMEM)
    hbm = pl.BlockSpec(memory_space=pl.ANY)
    flops = 3 * 2 * kmap.size // 2 * rows * channels * channels
    return pl.pallas_call(
        pair_kernel,
        out_shape=(
            jax.ShapeDtypeStruct((own_total, rows, channels), BF16),
            jax.ShapeDtypeStruct((ghost_total, rows, channels), BF16),
            jax.ShapeDtypeStruct((own_total, rows, channels), F32),
            jax.ShapeDtypeStruct((taps, channels, channels), BF16),
        ),
        in_specs=[smem, smem, hbm, hbm, vmem, hbm],
        out_specs=(vmem, vmem, vmem, vmem),
        scratch_shapes=[
            pltpu.VMEM((pool_total + 1, rows, channels), BF16),
            pltpu.VMEM((own_total + 1, rows, channels), F32),
            pltpu.VMEM((pool_total + 1, rows, channels), F32),
            pltpu.VMEM((taps, channels, channels), BF16),
            pltpu.SemaphoreType.DMA((3,)),
        ],
        cost_estimate=pl.CostEstimate(flops=flops, bytes_accessed=16 * 2 ** 20, transcendentals=0),
        compiler_params=pltpu.CompilerParams(vmem_limit_bytes=58 * 2 ** 20),
        name="pair_products",
    )(kmap.reshape(-1), counts, own, incoming, upstream, weights)


def reduce_kernel(wgrad_ref, ghost_ref, whole_ref, returned_ref,
                  near, far, crossed, portion, pieces, acc, total,
                  near_sems, far_sems, piece_sems, whole_sems, ghost_sems, local_sems):
    peers = lax.axis_size("dp")
    me = lax.axis_index("dp")
    column = lax.axis_index("fsdp")
    sibling = column + 1 - 2 * lax.rem(column, 2)
    across = column + 2 - 4 * lax.rem(lax.div(column, 2), 2)
    diagonal = sibling + 2 - 4 * lax.rem(lax.div(sibling, 2), 2)
    taps, depth, _ = far.shape
    share = total.shape[0]
    cap = ghost_ref.shape[0] // peers

    def peer_of(step):
        return lax.rem(me + step, peers)

    barrier = pltpu.get_barrier_semaphore()

    def greet(step, carry):
        pl.semaphore_signal(barrier, inc=1, device_id=(peer_of(step), column),
                            device_id_type=pl.DeviceIdType.MESH)
        return carry

    for other in (sibling, across):
        pl.semaphore_signal(barrier, inc=1, device_id=(me, other),
                            device_id_type=pl.DeviceIdType.MESH)
    lax.fori_loop(1, peers, greet, 0)
    pl.semaphore_wait(barrier, peers + 1)

    def remote(source, target, sems, step, device):
        return pltpu.make_async_remote_copy(
            src_ref=source, dst_ref=target, send_sem=sems.at[0, step], recv_sem=sems.at[1, step],
            device_id=device, device_id_type=pl.DeviceIdType.MESH)

    def shard(index):
        return wgrad_ref.at[:, pl.ds(pl.multiple_of(index * depth, depth), depth), :]

    to_far = remote(shard(diagonal), near.at[1], near_sems, 1, (me, sibling))
    to_near = remote(shard(sibling), near.at[0], near_sems, 0, (me, sibling))
    to_far.start()
    to_near.start()

    def ghost_copy(step):
        peer = peer_of(step)
        return remote(ghost_ref.at[pl.ds(peer * cap, cap)], returned_ref.at[pl.ds(me * cap, cap)],
                      ghost_sems, step, (peer, column))

    def piece_copy(step):
        peer = peer_of(step)
        return remote(portion.at[pl.ds(pl.multiple_of(peer * share, 16), share)], pieces.at[step],
                      piece_sems, step, (peer, column))

    def whole_copy(step):
        return remote(total, whole_ref.at[pl.ds(pl.multiple_of(me * share, 16), share)],
                      whole_sems, step, (peer_of(step), column))

    def begin(copy):
        def go(step, carry):
            copy(step).start()
            return carry
        lax.fori_loop(1, peers, go, 0)

    def finish(copy):
        def go(step, carry):
            copy(step).wait()
            return carry
        lax.fori_loop(1, peers, go, 0)

    begin(ghost_copy)
    kept = pltpu.make_async_copy(ghost_ref.at[pl.ds(me * cap, cap)],
                                 returned_ref.at[pl.ds(me * cap, cap)], local_sems.at[0])
    kept.start()

    def load(index, t):
        return wgrad_ref[t, pl.ds(pl.multiple_of(index * depth, depth), depth), :].astype(F32)

    to_far.wait()

    def far_sum(t, carry):
        far[t] = (load(across, t) + near[1, t].astype(F32)).astype(BF16)
        return carry

    lax.fori_loop(0, taps, far_sum, 0)
    to_across = remote(far, crossed, far_sems, 0, (me, across))
    to_across.start()
    padding = portion.shape[0] - taps * depth
    if padding:
        portion[pl.ds(taps * depth, padding), :] = jnp.zeros((padding, portion.shape[1]), BF16)
    to_near.wait()
    to_across.wait()

    def near_sum(t, carry):
        value = load(column, t) + near[0, t].astype(F32) + crossed[t].astype(F32)
        portion[pl.ds(pl.multiple_of(t * depth, depth), depth), :] = value.astype(BF16)
        return carry

    lax.fori_loop(0, taps, near_sum, 0)
    begin(piece_copy)
    acc[...] = portion[pl.ds(pl.multiple_of(me * share, 16), share), :].astype(F32)

    def add_piece(step, carry):
        piece_copy(step).wait()
        acc[...] += pieces[step].astype(F32)
        return carry

    lax.fori_loop(1, peers, add_piece, 0)
    total[...] = acc[...].astype(BF16)
    begin(whole_copy)
    mine = pltpu.make_async_copy(
        total, whole_ref.at[pl.ds(pl.multiple_of(me * share, 16), share)], local_sems.at[1])
    mine.start()
    mine.wait()
    kept.wait()
    finish(ghost_copy)
    finish(whole_copy)


def reduce_and_return(wgrad, ghosts, peers, depth):
    taps, _, channels = wgrad.shape
    share = -(-taps * depth // (16 * peers)) * 16
    vmem = pl.BlockSpec(memory_space=pltpu.VMEM)
    hbm = pl.BlockSpec(memory_space=pl.ANY)
    return pl.pallas_call(
        reduce_kernel,
        out_shape=(
            jax.ShapeDtypeStruct((share * peers, channels), BF16),
            jax.ShapeDtypeStruct(ghosts.shape, BF16),
        ),
        in_specs=[vmem, hbm],
        out_specs=(hbm, hbm),
        scratch_shapes=[
            pltpu.VMEM((2, taps, depth, channels), BF16),
            pltpu.VMEM((taps, depth, channels), BF16),
            pltpu.VMEM((taps, depth, channels), BF16),
            pltpu.VMEM((share * peers, channels), BF16),
            pltpu.VMEM((peers, share, channels), BF16),
            pltpu.VMEM((share, channels), F32),
            pltpu.VMEM((share, channels), BF16),
            pltpu.SemaphoreType.DMA((2, 2)),
            pltpu.SemaphoreType.DMA((2, 1)),
            pltpu.SemaphoreType.DMA((2, peers)),
            pltpu.SemaphoreType.DMA((2, peers)),
            pltpu.SemaphoreType.DMA((2, peers)),
            pltpu.SemaphoreType.DMA((2,)),
        ],
        compiler_params=pltpu.CompilerParams(
            collective_id=0, has_side_effects=True, vmem_limit_bytes=40 * 2 ** 20),
        name="reduce_and_return",
    )(wgrad, ghosts)


def on_device(feats, grad_out, kernel, send_bricks, kmap, pair_count):
    own = feats[0, 0]
    senders = send_bricks[0, 0]
    peers, cap = senders.shape
    own_total, rows, channels = own.shape
    taps, depth, _ = kernel.shape
    filled = senders >= 0
    outgoing = own[jnp.maximum(senders, 0)] * filled[:, :, None, None].astype(BF16)
    incoming = lax.all_to_all(outgoing, "dp", split_axis=0, concat_axis=0, tiled=True)
    weights = lax.all_gather(kernel, "fsdp", axis=1, tiled=True)
    produced, ghosts, own_grad, wgrad = pair_products(
        kmap[0, 0], pair_count[0, 0], own, incoming.reshape(peers * cap, rows, channels),
        grad_out[0, 0], weights)
    whole, returned = reduce_and_return(wgrad, ghosts, peers, depth)
    chosen = (senders.reshape(1, -1) == jnp.arange(own_total)[:, None]).astype(BF16)
    back = jnp.einsum("bk,kvc->bvc", chosen, returned,
                      preferred_element_type=F32)
    in_grad = (own_grad + back).astype(BF16)
    divisor = F32(4 * lax.axis_size("dp") * lax.axis_size("fsdp"))
    kernel_grad = whole[:taps * depth].reshape(taps, depth, channels).astype(F32) / divisor
    return (produced[None, None], in_grad[None, None], kernel_grad)


def solution(mesh):
    bricks = P("dp", "fsdp", None, None, None)
    return jax.shard_map(
        on_device,
        mesh=mesh,
        in_specs=(bricks, bricks, P(None, "fsdp", None), P("dp", "fsdp", None, None),
                  P("dp", "fsdp", None, None, None), P("dp", "fsdp", None)),
        out_specs=(bricks, bricks, P(None, "fsdp", None)),
        check_vma=False,
    )
```

```python
import jax
import jax.numpy as jnp
from jax import lax
from jax.experimental import pallas as pl
from jax.experimental.pallas import tpu as pltpu
from jax.sharding import PartitionSpec as P

F32 = jnp.float32
BF16 = jnp.bfloat16


def pair_kernel(kmap_ref, count_ref, own_ref, incoming_ref, upstream_ref, weights_ref,
                out_ref, ghost_ref, own_grad_ref, wgrad_ref,
                pool, out_acc, pool_acc, weights, sems):
    taps = weights.shape[0]
    slots = kmap_ref.shape[0] // (2 * taps)
    own_total = own_ref.shape[0]
    pool_total = pool.shape[0] - 1
    copies = [
        pltpu.make_async_copy(own_ref, pool.at[pl.ds(0, own_total)], sems.at[0]),
        pltpu.make_async_copy(incoming_ref, pool.at[pl.ds(own_total, pool_total - own_total)], sems.at[1]),
        pltpu.make_async_copy(weights_ref, weights, sems.at[2]),
    ]
    for copy in copies:
        copy.start()
    pool[pool_total] = jnp.zeros(pool.shape[1:], BF16)
    out_acc[...] = jnp.zeros_like(out_acc)
    pool_acc[...] = jnp.zeros_like(pool_acc)
    for copy in copies:
        copy.wait()

    def tap_step(t, carry):
        count = count_ref[t]
        sources, targets = [], []
        for s in range(slots):
            live = s < count
            sources.append(jnp.where(live, kmap_ref[t * 2 * slots + s], pool_total))
            targets.append(jnp.where(live, kmap_ref[t * 2 * slots + slots + s], own_total))
        inputs = jnp.concatenate([pool[i] for i in sources], axis=0)
        upstream = jnp.concatenate(
            [upstream_ref[jnp.minimum(o, own_total - 1)] for o in targets], axis=0)
        tap = weights[t]
        forward = jnp.dot(inputs, tap, preferred_element_type=F32)
        backward = lax.dot_general(upstream, tap, (((1,), (1,)), ((), ())), preferred_element_type=F32)
        wgrad = lax.dot_general(inputs, upstream, (((0,), (0,)), ((), ())), preferred_element_type=F32)
        wgrad_ref[t] = wgrad.astype(BF16)
        rows = pool.shape[1]
        for s in range(slots):
            out_acc[targets[s]] += forward[s * rows:(s + 1) * rows]
            pool_acc[sources[s]] += backward[s * rows:(s + 1) * rows]
        return carry

    lax.fori_loop(0, taps, tap_step, 0)
    out_ref[...] = out_acc[:own_total].astype(BF16)
    own_grad_ref[...] = pool_acc[:own_total]
    ghost_ref[...] = pool_acc[own_total:pool_total].astype(BF16)


def pair_products(kmap, counts, own, incoming, upstream, weights):
    own_total, rows, channels = own.shape
    ghost_total = incoming.shape[0]
    taps = weights.shape[0]
    pool_total = own_total + ghost_total
    smem = pl.BlockSpec(memory_space=pltpu.SMEM)
    vmem = pl.BlockSpec(memory_space=pltpu.VMEM)
    hbm = pl.BlockSpec(memory_space=pl.ANY)
    flops = 3 * 2 * kmap.size // 2 * rows * channels * channels
    return pl.pallas_call(
        pair_kernel,
        out_shape=(
            jax.ShapeDtypeStruct((own_total, rows, channels), BF16),
            jax.ShapeDtypeStruct((ghost_total, rows, channels), BF16),
            jax.ShapeDtypeStruct((own_total, rows, channels), F32),
            jax.ShapeDtypeStruct((taps, channels, channels), BF16),
        ),
        in_specs=[smem, smem, hbm, hbm, vmem, hbm],
        out_specs=(vmem, vmem, vmem, vmem),
        scratch_shapes=[
            pltpu.VMEM((pool_total + 1, rows, channels), BF16),
            pltpu.VMEM((own_total + 1, rows, channels), F32),
            pltpu.VMEM((pool_total + 1, rows, channels), F32),
            pltpu.VMEM((taps, channels, channels), BF16),
            pltpu.SemaphoreType.DMA((3,)),
        ],
        cost_estimate=pl.CostEstimate(flops=flops, bytes_accessed=16 * 2 ** 20, transcendentals=0),
        compiler_params=pltpu.CompilerParams(vmem_limit_bytes=58 * 2 ** 20),
        name="pair_products",
    )(kmap.reshape(-1), counts, own, incoming, upstream, weights)


def reduce_kernel(wgrad_ref, ghost_ref, whole_ref, returned_ref,
                  near, far, crossed, portion, pieces, acc, total,
                  near_sems, far_sems, piece_sems, whole_sems, ghost_sems, local_sems):
    peers = lax.axis_size("dp")
    me = lax.axis_index("dp")
    column = lax.axis_index("fsdp")
    sibling = column + 1 - 2 * lax.rem(column, 2)
    across = column + 2 - 4 * lax.rem(lax.div(column, 2), 2)
    diagonal = sibling + 2 - 4 * lax.rem(lax.div(sibling, 2), 2)
    taps, depth, _ = far.shape
    share = total.shape[0]
    cap = ghost_ref.shape[0] // peers

    def peer_of(step):
        return lax.rem(me + step, peers)

    barrier = pltpu.get_barrier_semaphore()

    def greet(step, carry):
        pl.semaphore_signal(barrier, inc=1, device_id=(peer_of(step), column),
                            device_id_type=pl.DeviceIdType.MESH)
        return carry

    for other in (sibling, across):
        pl.semaphore_signal(barrier, inc=1, device_id=(me, other),
                            device_id_type=pl.DeviceIdType.MESH)
    lax.fori_loop(1, peers, greet, 0)
    pl.semaphore_wait(barrier, peers + 1)

    def remote(source, target, sems, step, device):
        return pltpu.make_async_remote_copy(
            src_ref=source, dst_ref=target, send_sem=sems.at[0, step], recv_sem=sems.at[1, step],
            device_id=device, device_id_type=pl.DeviceIdType.MESH)

    def shard(index):
        return wgrad_ref.at[:, pl.ds(pl.multiple_of(index * depth, depth), depth), :]

    to_far = remote(shard(diagonal), near.at[1], near_sems, 1, (me, sibling))
    to_near = remote(shard(sibling), near.at[0], near_sems, 0, (me, sibling))
    to_far.start()
    to_near.start()

    def ghost_copy(step):
        peer = peer_of(step)
        return remote(ghost_ref.at[pl.ds(peer * cap, cap)], returned_ref.at[pl.ds(me * cap, cap)],
                      ghost_sems, step, (peer, column))

    def piece_copy(step):
        peer = peer_of(step)
        return remote(portion.at[pl.ds(pl.multiple_of(peer * share, 16), share)], pieces.at[step],
                      piece_sems, step, (peer, column))

    def whole_copy(step):
        return remote(total, whole_ref.at[pl.ds(pl.multiple_of(me * share, 16), share)],
                      whole_sems, step, (peer_of(step), column))

    def begin(copy):
        def go(step, carry):
            copy(step).start()
            return carry
        lax.fori_loop(1, peers, go, 0)

    def finish(copy):
        def go(step, carry):
            copy(step).wait()
            return carry
        lax.fori_loop(1, peers, go, 0)

    begin(ghost_copy)
    kept = pltpu.make_async_copy(ghost_ref.at[pl.ds(me * cap, cap)],
                                 returned_ref.at[pl.ds(me * cap, cap)], local_sems.at[0])
    kept.start()

    def load(index, t):
        return wgrad_ref[t, pl.ds(pl.multiple_of(index * depth, depth), depth), :].astype(F32)

    to_far.wait()

    def far_sum(t, carry):
        far[t] = (load(across, t) + near[1, t].astype(F32)).astype(BF16)
        return carry

    lax.fori_loop(0, taps, far_sum, 0)
    to_across = remote(far, crossed, far_sems, 0, (me, across))
    to_across.start()
    padding = portion.shape[0] - taps * depth
    if padding:
        portion[pl.ds(taps * depth, padding), :] = jnp.zeros((padding, portion.shape[1]), BF16)
    to_near.wait()
    to_across.wait()

    def near_sum(t, carry):
        value = load(column, t) + near[0, t].astype(F32) + crossed[t].astype(F32)
        portion[pl.ds(pl.multiple_of(t * depth, depth), depth), :] = value.astype(BF16)
        return carry

    lax.fori_loop(0, taps, near_sum, 0)
    begin(piece_copy)
    acc[...] = portion[pl.ds(pl.multiple_of(me * share, 16), share), :].astype(F32)

    def add_piece(step, carry):
        piece_copy(step).wait()
        acc[...] += pieces[step].astype(F32)
        return carry

    lax.fori_loop(1, peers, add_piece, 0)
    total[...] = acc[...].astype(BF16)
    begin(whole_copy)
    mine = pltpu.make_async_copy(
        total, whole_ref.at[pl.ds(pl.multiple_of(me * share, 16), share)], local_sems.at[1])
    mine.start()
    mine.wait()
    kept.wait()
    finish(ghost_copy)
    finish(whole_copy)


def reduce_and_return(wgrad, ghosts, peers, depth):
    taps, _, channels = wgrad.shape
    share = -(-taps * depth // (16 * peers)) * 16
    vmem = pl.BlockSpec(memory_space=pltpu.VMEM)
    hbm = pl.BlockSpec(memory_space=pl.ANY)
    return pl.pallas_call(
        reduce_kernel,
        out_shape=(
            jax.ShapeDtypeStruct((share * peers, channels), BF16),
            jax.ShapeDtypeStruct(ghosts.shape, BF16),
        ),
        in_specs=[vmem, hbm],
        out_specs=(hbm, hbm),
        scratch_shapes=[
            pltpu.VMEM((2, taps, depth, channels), BF16),
            pltpu.VMEM((taps, depth, channels), BF16),
            pltpu.VMEM((taps, depth, channels), BF16),
            pltpu.VMEM((share * peers, channels), BF16),
            pltpu.VMEM((peers, share, channels), BF16),
            pltpu.VMEM((share, channels), F32),
            pltpu.VMEM((share, channels), BF16),
            pltpu.SemaphoreType.DMA((2, 2)),
            pltpu.SemaphoreType.DMA((2, 1)),
            pltpu.SemaphoreType.DMA((2, peers)),
            pltpu.SemaphoreType.DMA((2, peers)),
            pltpu.SemaphoreType.DMA((2, peers)),
            pltpu.SemaphoreType.DMA((2,)),
        ],
        compiler_params=pltpu.CompilerParams(
            collective_id=0, has_side_effects=True, vmem_limit_bytes=40 * 2 ** 20),
        name="reduce_and_return",
    )(wgrad, ghosts)


def gather_kernel(senders_ref, own_ref, kernel_ref, incoming_ref, weights_ref,
                  outgoing, weight_sems, brick_sems, local_sems):
    peers = lax.axis_size("dp")
    me = lax.axis_index("dp")
    column = lax.axis_index("fsdp")
    sibling = column + 1 - 2 * lax.rem(column, 2)
    across = column + 2 - 4 * lax.rem(lax.div(column, 2), 2)
    depth = kernel_ref.shape[1]
    cap = outgoing.shape[0] // peers

    def peer_of(step):
        return lax.rem(me + step, peers)

    barrier = pltpu.get_barrier_semaphore()

    def greet(step, carry):
        pl.semaphore_signal(barrier, inc=1, device_id=(peer_of(step), column),
                            device_id_type=pl.DeviceIdType.MESH)
        return carry

    for other in (sibling, across):
        pl.semaphore_signal(barrier, inc=1, device_id=(me, other),
                            device_id_type=pl.DeviceIdType.MESH)
    lax.fori_loop(1, peers, greet, 0)
    pl.semaphore_wait(barrier, peers + 1)

    def shard(index):
        return weights_ref.at[:, pl.ds(pl.multiple_of(index * depth, depth), depth), :]

    def remote(source, target, sems, step, device):
        return pltpu.make_async_remote_copy(
            src_ref=source, dst_ref=target, send_sem=sems.at[0, step], recv_sem=sems.at[1, step],
            device_id=device, device_id_type=pl.DeviceIdType.MESH)

    to_across = remote(kernel_ref, shard(column), weight_sems, 0, (me, across))
    to_sibling = remote(kernel_ref, shard(column), weight_sems, 1, (me, sibling))
    to_across.start()
    to_sibling.start()
    kept = pltpu.make_async_copy(kernel_ref, shard(column), local_sems.at[0])
    kept.start()

    def fill(peer):
        for c in range(cap):
            brick = senders_ref[peer * cap + c]
            mask = (brick >= 0).astype(F32)
            value = own_ref[jnp.maximum(brick, 0)].astype(F32) * mask
            outgoing[peer * cap + c] = value.astype(BF16)

    def brick_copy(step):
        peer = peer_of(step)
        return remote(outgoing.at[pl.ds(peer * cap, cap)], incoming_ref.at[pl.ds(me * cap, cap)],
                      brick_sems, step, (peer, column))

    def send(step, carry):
        fill(peer_of(step))
        brick_copy(step).start()
        return carry

    lax.fori_loop(1, peers, send, 0)
    fill(me)
    mine = pltpu.make_async_copy(outgoing.at[pl.ds(me * cap, cap)],
                                 incoming_ref.at[pl.ds(me * cap, cap)], local_sems.at[1])
    mine.start()
    to_across.wait()
    forward = remote(shard(across), shard(across), weight_sems, 2, (me, sibling))
    forward.start()
    to_sibling.wait()
    kept.wait()
    mine.wait()

    def finish(step, carry):
        brick_copy(step).wait()
        return carry

    lax.fori_loop(1, peers, finish, 0)
    forward.wait()


def gather_inputs(senders, own, kernel, columns):
    peers, cap = senders.shape
    taps, depth, channels = kernel.shape
    bricks = (peers * cap,) + own.shape[1:]
    hbm = pl.BlockSpec(memory_space=pl.ANY)
    return pl.pallas_call(
        gather_kernel,
        out_shape=(
            jax.ShapeDtypeStruct(bricks, BF16),
            jax.ShapeDtypeStruct((taps, depth * columns, channels), BF16),
        ),
        in_specs=[pl.BlockSpec(memory_space=pltpu.SMEM),
                  pl.BlockSpec(memory_space=pltpu.VMEM), hbm],
        out_specs=(hbm, hbm),
        scratch_shapes=[
            pltpu.VMEM(bricks, BF16),
            pltpu.SemaphoreType.DMA((2, 3)),
            pltpu.SemaphoreType.DMA((2, peers)),
            pltpu.SemaphoreType.DMA((2,)),
        ],
        compiler_params=pltpu.CompilerParams(
            collective_id=1, has_side_effects=True, vmem_limit_bytes=40 * 2 ** 20),
        name="gather_inputs",
    )(senders.reshape(-1), own, kernel)


def on_device(feats, grad_out, kernel, send_bricks, kmap, pair_count):
    own = feats[0, 0]
    senders = send_bricks[0, 0]
    peers = senders.shape[0]
    own_total, _, channels = own.shape
    taps, depth, _ = kernel.shape
    incoming, weights = gather_inputs(senders, own, kernel, lax.axis_size("fsdp"))
    produced, ghosts, own_grad, wgrad = pair_products(
        kmap[0, 0], pair_count[0, 0], own, incoming,
        grad_out[0, 0], weights)
    whole, returned = reduce_and_return(wgrad, ghosts, peers, depth)
    chosen = (senders.reshape(1, -1) == jnp.arange(own_total)[:, None]).astype(BF16)
    back = jnp.einsum("bk,kvc->bvc", chosen, returned,
                      preferred_element_type=F32)
    in_grad = (own_grad + back).astype(BF16)
    divisor = F32(4 * lax.axis_size("dp") * lax.axis_size("fsdp"))
    kernel_grad = whole[:taps * depth].reshape(taps, depth, channels).astype(F32) / divisor
    return (produced[None, None], in_grad[None, None], kernel_grad)


def solution(mesh):
    bricks = P("dp", "fsdp", None, None, None)
    return jax.shard_map(
        on_device,
        mesh=mesh,
        in_specs=(bricks, bricks, P(None, "fsdp", None), P("dp", "fsdp", None, None),
                  P("dp", "fsdp", None, None, None), P("dp", "fsdp", None)),
        out_specs=(bricks, bricks, P(None, "fsdp", None)),
        check_vma=False,
    )
```
